32 devices in a mesh: groups: 2 (over y), pool: 4 (over z), tensor: 4 (over x, core).
Axes of the slice: x: 2, y: 2, z: 4, core: 2. Of those that a mesh axis runs over, the one named last changes fastest.
Arguments:
- tokens: bfloat16 [256, 4096], P(('groups', 'pool'), 'tensor'), parts along dimension 0, may hold values from -6 to 6
- route_ids: int32 [256, 8], P(('groups', 'pool')), parts along dimension 0, may hold values from 0 to 63, all different within a row; in each aligned block of 32 rows (0 to 31, 32 to 63, ...) at most 6 rows name the same one
- route_weights: float32 [256, 8], P(('groups', 'pool')), parts along dimension 0, may hold values from 0.03 to 0.6
- gate_weight: bfloat16 [64, 4096, 768], P('pool', None, 'tensor'), may hold values from -0.09375 to 0.09375
- up_weight: bfloat16 [64, 4096, 768], P('pool', None, 'tensor'), may hold values from -0.09375 to 0.09375
- down_weight: bfloat16 [64, 768, 4096], P('pool', 'tensor'), may hold values from -0.21875 to 0.21875
- queries: bfloat16 [32, 4, 16, 128], P(('groups', 'pool'), 'tensor'), parts along dimension 0, may hold values from -160 to 160
- keys: bfloat16 [32, 4, 128, 128], P(('groups', 'pool'), 'tensor'), parts along dimension 0, may hold values from -6 to 6
- values: bfloat16 [32, 4, 128, 128], P(('groups', 'pool'), 'tensor'), parts along dimension 0, may hold values from -6 to 6
- lengths: int32 [32], P(('groups', 'pool')), parts along dimension 0, may hold values from 1 to 128, as said below
Outputs:
- attention: bfloat16 [32, 4, 16, 128], P(('groups', 'pool')), parts along dimension 0
- combined: bfloat16 [256, 4096], P(('groups', 'pool'), 'tensor'), parts along dimension 0
The draws below stay inside these ranges and needn't reach their ends.
There are 2 independent parts, one for each index of `groups`. The reference program is written for one: setup_inputs(seed, part) draws one part's arguments, and reference() takes and returns one part's arrays. A program takes and returns all parts, laid end to end along the dimension named above; an argument that names none is the same for every part. Nothing has to cross between parts.
Inputs may be any that keep to these rules, and one draw needn't show every extreme that they name: `route_ids`: each row names 8 different experts; among the 32 tokens of one index of pool no expert is named more than 6 times, a bound that some block reaches. `lengths`: the first sequence has all 128 positions live.
All inputs are finite; a program needn't handle non-finite values.
Results may differ from the reference program's by a relative error of at most 0.014.
Values may be sent and summed in bfloat16 or wider, within the bound.
A program may use at most 192 MiB of HBM per device.

```python
import math
import jax
import jax.numpy as jnp
import numpy as np
from jax import lax

D = 4096
KVH = 4
HD = 128
TOP = 8
EXPERTS = 64
FF = 768
TOK_DEV = 32
CTX = 128
GQ = 16
CAP = 6
TOKENS = 128
SEQS = 16
N_POOL = 4
N_TENSOR = 4


def shared_keys(key):
    return jnp.clip(jax.random.normal(jax.random.fold_in(key, 17), (SEQS, KVH, CTX, HD), jnp.float32), -6.0, 6.0)


def draw_keys(key, part):
    cached = shared_keys(key)
    return cached.astype(jnp.bfloat16)


def draw_queries(key, part):
    key = jax.random.fold_in(key, 2)
    asked = jnp.clip(jax.random.normal(key, (SEQS, KVH, GQ, HD), jnp.float32), -6.0, 6.0)
    return asked.astype(jnp.bfloat16)


def draw_lengths(key, part):
    key = jax.random.fold_in(key, 3)
    drawn = jax.random.randint(key, (SEQS,), 1, CTX + 1, jnp.int32)
    return drawn.at[0].set(CTX)


def shard_levels(key, dims, shards, smallest, largest):
    gain, own = 1.0, jax.random.fold_in(key, 6)
    for dim, blocks in shards:
        heights = jnp.exp(jax.random.uniform(jax.random.fold_in(own, dim), (blocks,), jnp.float32, smallest / len(shards), largest / len(shards)))
        gain = gain * jnp.repeat(heights, dims[dim] // blocks).reshape([-1 if axis == dim else 1 for axis in range(len(dims))])
    return gain


def routed_block(stream_key, own, number, rows, count, top, most, slope):
    ranking = jax.random.permutation(stream_key, count)
    crowded, common = portions_of(count, rows * top, most, slope, True), portions_of(count, rows * top, most, slope, False)
    places = jnp.arange(count)

    def named(sizes, offset_by):
        used = int((sizes > 0).sum())
        fixed = max(1, used // 4)
        shifted = fixed + (places - fixed + offset_by * (used - fixed)) % max(1, count - fixed)
        return jnp.zeros((count,), jnp.int32).at[ranking[jnp.where(places < fixed, places, shifted)]].set(jnp.asarray(sizes, jnp.int32))

    sizes = jnp.where(number % 4 == 0, named(crowded, number // 4), named(common, number - number // 4 - 1))
    mixed = jax.random.permutation(jax.random.fold_in(own, 3), count)
    donor, taker = mixed[0:count // 2 * 2:2], mixed[1:count // 2 * 2:2]
    margin = jnp.minimum(sizes[donor] - 1, most - sizes[taker]) // 2
    margin = jnp.where((donor == ranking[0]) | (taker == ranking[0]) | (sizes[taker] == 0), 0, jnp.maximum(margin, 0))
    shifted = jax.random.randint(jax.random.fold_in(own, 4), (count // 2,), 0, 1 << 20) % (margin + 1)
    sizes = sizes.at[donor].add(-shifted).at[taker].add(shifted)
    labels = jnp.searchsorted(jnp.cumsum(sizes), jnp.arange(rows * top), side="right").astype(jnp.int32)
    grid = labels.reshape(top, rows).T
    grid = grid[jax.random.permutation(jax.random.fold_in(own, 1), rows)]
    offset_by = jax.random.randint(jax.random.fold_in(own, 2), (rows, 1), 0, top)
    return jnp.take_along_axis(grid, (jnp.arange(top)[None, :] + offset_by) % top, axis=1)


def portions_of(count, total, most, skew, full):
    weights = [(1 << 20) // math.isqrt(grade ** skew) + 1 for grade in range(1, count + 1)]
    largest = most if full else min(most, max(-(-total // count), total * weights[0] // sum(weights)))
    least = 1 if total - largest >= count - 1 else 0
    holding, surplus = [largest] + [least] * (count - 1), total - largest - least * (count - 1)
    while surplus > 0:
        movable = [i for i in range(1, count) if holding[i] < largest] or [i for i in range(1, count) if holding[i] < most]
        pool, budget = sum([weights[i] for i in movable]), surplus
        for i in movable:
            more = min(most - holding[i], max(1, budget * weights[i] // pool), surplus)
            holding[i] = holding[i] + more
            surplus = surplus - more
    return np.array(holding)


def noise(rng, shape, deviation, bound, shards=(), kind=jnp.bfloat16):
    level = shard_levels(rng, shape, shards, -0.22, 0.18) if shards else 1.0
    values = jax.random.normal(rng, shape, jnp.float32) * deviation * level
    return jnp.minimum(jnp.maximum(values, -bound), bound).astype(kind)


def setup_inputs(seed: int = 0, part: int = 0) -> dict:
    arg_keys = jax.random.split(jax.random.key(seed), 11)
    own_keys = jax.random.split(jax.random.fold_in(arg_keys[10], part), 11)
    tokens = noise(own_keys[0], (TOKENS, D), 1.0, 6.0, ((0, 4), (1, 4)))
    route_ids_keys = jax.random.split(jax.random.fold_in(own_keys[1], 1), TOKENS // TOK_DEV)
    route_ids_turns = jax.random.permutation(jax.random.fold_in(own_keys[1], 3), TOKENS // TOK_DEV)
    route_ids = jax.vmap(lambda own, number: routed_block(jax.random.fold_in(own_keys[1], 2), own, number, TOK_DEV, EXPERTS, TOP, CAP, 2))(route_ids_keys, route_ids_turns).reshape((TOKENS, TOP))
    route_weights = jnp.clip(jnp.exp(math.log(0.6) - 2.9957323 * jax.random.uniform(own_keys[2], (TOKENS, TOP), jnp.float32) ** shard_levels(own_keys[2], (TOKENS, TOP), ((0, 4),), -0.2, 0.2)), 0.03, 0.6)
    gate_weight = noise(arg_keys[3], (EXPERTS, D, FF), D ** -0.5, 0.09375, ((0, 4), (2, 4)))
    up_weight = noise(arg_keys[4], (EXPERTS, D, FF), D ** -0.5, 0.09375, ((0, 4), (2, 4)))
    down_weight = noise(arg_keys[5], (EXPERTS, FF, D), FF ** -0.5, 0.21875, ((0, 4), (1, 4)))
    queries = draw_queries(jax.random.fold_in(jax.random.fold_in(arg_keys[10], part), 71), part)
    keys = draw_keys(jax.random.fold_in(jax.random.fold_in(arg_keys[10], part), 71), part)
    values = noise(own_keys[8], (SEQS, KVH, CTX, HD), 1.0, 6.0, ((0, 4), (1, 4)))
    lengths = draw_lengths(jax.random.fold_in(jax.random.fold_in(arg_keys[10], part), 71), part)
    return dict(tokens=tokens, route_ids=route_ids, route_weights=route_weights, gate_weight=gate_weight, up_weight=up_weight, down_weight=down_weight, queries=queries, keys=keys, values=values, lengths=lengths)


def attend(queries, keys, values, lengths):
    scale = HD ** -0.5
    scores = jnp.einsum("sjgh,sjch->sjgc", queries.astype(jnp.float32), keys.astype(jnp.float32)) * scale
    position = jnp.arange(CTX, dtype=jnp.int32)
    live = position[None, :] < lengths[:, None]
    scores = jnp.where(live[:, None, None, :], scores, -1e30)
    highest = jnp.max(scores, axis=3, keepdims=True)
    probs = jnp.exp(scores - highest)
    weights = (probs / jnp.sum(probs, axis=3, keepdims=True)).astype(jnp.bfloat16)
    mixed = jnp.einsum("sjgc,sjch->sjgh", weights.astype(jnp.float32), values.astype(jnp.float32))
    return mixed.astype(jnp.bfloat16)


def expert_rows(rows, gate_w, up_w, down_w):
    gate = jnp.dot(rows, gate_w, preferred_element_type=jnp.float32)
    up = jnp.dot(rows, up_w, preferred_element_type=jnp.float32)
    hidden = (jax.nn.silu(gate) * up).astype(jnp.bfloat16)
    groups = hidden.reshape(rows.shape[0], N_TENSOR, FF // N_TENSOR).astype(jnp.float32)
    down_groups = down_w.reshape(N_TENSOR, FF // N_TENSOR, D).astype(jnp.float32)
    parts = jnp.einsum("rtf,tfd->trd", groups, down_groups)
    return jnp.sum(parts.astype(jnp.bfloat16).astype(jnp.float32), axis=0).astype(jnp.bfloat16)


def reference(tokens, route_ids, route_weights, gate_weight, up_weight, down_weight, queries, keys, values, lengths):
    attention = attend(queries, keys, values, lengths)
    flat_ids = route_ids.reshape(-1)
    count = flat_ids.shape[0]
    owner = jnp.arange(count, dtype=jnp.int32) // TOP
    room = N_POOL * CAP

    def one(expert):
        pick = jnp.argsort((flat_ids != expert).astype(jnp.int32), stable=True)[:room].astype(jnp.int32)
        valid = flat_ids[pick] == expert
        rows = tokens[owner[pick]]
        result = expert_rows(rows, gate_weight[expert], up_weight[expert], down_weight[expert])
        return pick, jnp.where(valid[:, None], result, jnp.zeros((), result.dtype))

    picks, outputs = lax.map(one, jnp.arange(EXPERTS, dtype=jnp.int32))
    terms = jnp.zeros((count, D), jnp.float32).at[picks.reshape(-1)].add(outputs.reshape(-1, D).astype(jnp.float32))
    combined = jnp.sum(terms.reshape(-1, TOP, D) * route_weights[:, :, None], axis=1).astype(jnp.bfloat16)
    return attention, combined
```

```python
import functools

import jax
import jax.numpy as jnp
from jax import lax
from jax.experimental import pallas as pl
from jax.experimental.pallas import tpu as pltpu
from jax.sharding import PartitionSpec as P

CAP = 6
TILE = 256
SLOTS = 6
F32 = jnp.float32
BF16 = jnp.bfloat16
VMEM_LIMIT = 60 * 1024 * 1024


def attend(queries, keys, values, lengths):
    scale = queries.shape[-1] ** (-0.5)
    scores = (
        jnp.einsum("sjgh,sjch->sjgc", queries, keys, preferred_element_type=jnp.float32) * scale
    )
    position = lax.broadcasted_iota(jnp.int32, (keys.shape[0], keys.shape[2]), 1)
    live = position < lengths[:, None]
    scores = jnp.where(live[:, None, None, :], scores, -1e30)
    highest = jnp.max(scores, axis=3, keepdims=True)
    probs = jnp.exp(scores - highest)
    weights = (probs / jnp.sum(probs, axis=3, keepdims=True)).astype(jnp.bfloat16)
    mixed = jnp.einsum("sjgc,sjch->sjgh", weights, values, preferred_element_type=jnp.float32)
    return mixed.astype(jnp.bfloat16)


def slot_table(route_ids, experts, capacity):
    flat_ids = route_ids.reshape(-1)
    count = flat_ids.shape[0]
    onehot = (flat_ids[:, None] == lax.broadcasted_iota(jnp.int32, (1, experts), 1)).astype(
        jnp.int32
    )
    before = jnp.cumsum(onehot, axis=0) - onehot
    rank = jnp.sum(before * onehot, axis=1)
    slot = flat_ids * capacity + rank
    owner = lax.broadcasted_iota(jnp.int32, (count,), 0) // route_ids.shape[1]
    source = jnp.full((experts * capacity,), -1, jnp.int32).at[slot].set(owner)
    return (slot, source)


def routed_shards(
    tokens, route_ids, route_weights, gate_weight, up_weight, down_weight,
    queries, keys, values, lengths,
):
    local_heads = attend(queries, keys, values, lengths)
    attention = lax.all_gather(local_heads, "tensor", axis=1, tiled=True)
    pool_size = lax.axis_size("pool")
    local_experts = gate_weight.shape[0]
    experts = local_experts * pool_size
    slot, source = slot_table(route_ids, experts, CAP)
    filled = (source >= 0)[:, None]
    picked = jnp.maximum(source, 0)
    whole = lax.all_gather(tokens, "tensor", axis=1, tiled=True)
    outgoing = jnp.where(filled, whole[picked], jnp.zeros((), whole.dtype))
    outgoing = outgoing.reshape(pool_size, local_experts, CAP, whole.shape[1])
    arrived = lax.all_to_all(outgoing, "pool", split_axis=0, concat_axis=0, tiled=True)
    gate = jnp.einsum("pech,ehf->pecf", arrived, gate_weight, preferred_element_type=jnp.float32)
    up = jnp.einsum("pech,ehf->pecf", arrived, up_weight, preferred_element_type=jnp.float32)
    hidden = (jax.nn.silu(gate) * up).astype(jnp.bfloat16)
    partial_value = jnp.einsum(
        "pecf,efd->pecd", hidden, down_weight, preferred_element_type=jnp.float32
    )
    summed = lax.psum_scatter(
        partial_value.astype(jnp.bfloat16), "tensor", scatter_dimension=3, tiled=True
    )
    returned = lax.all_to_all(summed, "pool", split_axis=0, concat_axis=0, tiled=True)
    fetched = returned.reshape(experts * CAP, returned.shape[3])[slot]
    fetched = fetched.reshape(route_ids.shape[0], route_ids.shape[1], returned.shape[3])
    combined = jnp.sum(fetched.astype(jnp.float32) * route_weights[:, :, None], axis=1)
    return (attention, combined.astype(jnp.bfloat16))


def kernel(
    experts, len_ref, tok_ref, ids_ref, rw_ref, q_ref, k_ref, v_ref, gate_hbm, up_hbm, down_hbm,
    attn_ref, comb_ref,
    x, tab_out, tab_in, heads_own, heads_in, gbuf, ubuf, dbuf, hid, acc,
    c1_out, c1_in, x_out, x_in, c3_out, c3_in, z_out, z_in,
    w_sem, d_sem, s_sem, r_sem,
):
    pools = x.shape[1]
    rows = x.shape[2]
    width = x.shape[3]
    toks = pools * rows
    units = gate_hbm.shape[0]
    ff = units // experts
    tiles = units // TILE
    p = lax.axis_index("pool")
    t = lax.axis_index("tensor")
    core = t + 1 - 2 * (t % 2)
    across = (t + 2) % 4
    corner = (core + 2) % 4
    blocks = (corner, across, core, t)

    def weights(i, slot):
        at = pl.ds(pl.multiple_of(i * TILE, TILE), TILE)
        return (
            pltpu.make_async_copy(gate_hbm.at[at], gbuf.at[slot], w_sem.at[0, slot]),
            pltpu.make_async_copy(up_hbm.at[at], ubuf.at[slot], w_sem.at[1, slot]),
        )

    def down(n):
        at = pl.ds(pl.multiple_of(blocks[n] * width, width), width)
        return pltpu.make_async_copy(down_hbm.at[:, at], dbuf.at[n], d_sem.at[n])

    for i in range(min(SLOTS, tiles)):
        for copy in weights(i, i):
            copy.start()
    for n in range(4):
        down(n).start()

    barrier = pltpu.get_barrier_semaphore()
    for j in range(1, pools):
        pl.semaphore_signal(barrier, inc=1, device_id={"pool": (p + j) % pools})
    for j in range(1, 4):
        pl.semaphore_signal(barrier, inc=1, device_id={"tensor": (t + j) % 4})
    pl.semaphore_wait(barrier, pools + 2)

    count = [0]
    sent = []

    def send(src, dst, where):
        n = count[0]
        count[0] = n + 1
        copy = pltpu.make_async_remote_copy(
            src_ref=src, dst_ref=dst, send_sem=s_sem.at[n], recv_sem=r_sem.at[n], device_id=where
        )
        copy.start()
        sent.append(copy)
        return copy

    x[t, p] = tok_ref[...]
    z_copies = {}
    for j in (2, 1, 3):
        if j < pools:
            z_copies[j] = send(tok_ref, x.at[t, p], {"pool": (p + pools - j) % pools})
    x_copies = [send(tok_ref, x.at[t, p], {"tensor": across})]
    core_copies = [send(tok_ref, x.at[t, p], {"tensor": core})]

    per_pool = experts
    lane = lax.broadcasted_iota(jnp.int32, (rows, 128), 1)
    ids = ids_ref[...]
    rw = rw_ref[...]
    tab_copies = []
    for j in range(pools):
        owner = (p + pools - j) % pools
        total = jnp.zeros((rows, 128), F32)
        for k in range(ids.shape[1]):
            hit = (ids[:, k : k + 1] - owner * per_pool) == lane
            total = total + jnp.where(hit, rw[:, k : k + 1], 0.0)
        total = jnp.where(lane < per_pool, total, 0.0)
        if j == 0:
            tab_in[p] = total
        else:
            tab_out[j] = total
            tab_copies.append(send(tab_out.at[j], tab_in.at[p], {"pool": owner}))

    scale = q_ref.shape[-1] ** (-0.5)
    for s in range(q_ref.shape[0]):
        scores = (
            lax.dot_general(
                q_ref[s], k_ref[s], (((1,), (1,)), ((), ())), preferred_element_type=F32
            )
            * scale
        )
        position = lax.broadcasted_iota(jnp.int32, scores.shape, 1)
        scores = jnp.where(position < len_ref[s], scores, -1e30)
        probs = jnp.exp(scores - jnp.max(scores, axis=1, keepdims=True))
        mix = (probs / jnp.sum(probs, axis=1, keepdims=True)).astype(BF16)
        heads_own[s] = jnp.dot(mix, v_ref[s], preferred_element_type=F32).astype(BF16)
    heads_in[t] = heads_own[...]
    head_copies = [
        send(heads_own, heads_in.at[t], {"tensor": (t + j) % 4}) for j in range(1, 4)
    ]

    for j in (1, 3, 2):
        if j < pools:
            z_copies[j].wait_recv()
            block = x.at[t, (p + j) % pools]
            x_copies.append(send(block, block, {"tensor": across}))
            core_copies.append(send(block, block, {"tensor": core}))
    order = [0] + [j for j in (1, 3, 2) if j < pools]
    for n, j in enumerate(order):
        x_copies[n].wait_recv()
        block = x.at[across, (p + j) % pools]
        core_copies.append(send(block, block, {"tensor": core}))
    for copy in core_copies + tab_copies:
        copy.wait_recv()

    table = tab_in[...].reshape(toks, 128)
    wide_lane = lax.broadcasted_iota(jnp.int32, (toks, 128), 1)
    unit = lax.broadcasted_iota(jnp.int32, (toks, TILE), 1)

    def step(i, carry):
        slot = i % SLOTS
        for copy in weights(i, slot):
            copy.wait()
        gate = jnp.zeros((toks, TILE), F32)
        up = jnp.zeros((toks, TILE), F32)
        for b in range(4):
            xb = x[b].reshape(toks, width)
            at = slice(b * width, (b + 1) * width)
            dims = (((1,), (1,)), ((), ()))
            gate = gate + lax.dot_general(xb, gbuf[slot, :, at], dims, preferred_element_type=F32)
            up = up + lax.dot_general(xb, ubuf[slot, :, at], dims, preferred_element_type=F32)
        first = (i * TILE) // ff
        share = jnp.zeros((toks, TILE), F32)
        for m in range((TILE - 2) // ff + 2):
            e = first + m
            col = jnp.sum(jnp.where(wide_lane == e, table, 0.0), axis=1, keepdims=True)
            mine = (unit >= e * ff - i * TILE) & (unit < (e + 1) * ff - i * TILE)
            share = jnp.where(mine, col, share)
        value = gate / (1.0 + jnp.exp(-gate)) * up * share
        hid[:, pl.ds(pl.multiple_of(i * TILE, TILE), TILE)] = value.astype(BF16)

        @pl.when(i + SLOTS < tiles)
        def _():
            for copy in weights(i + SLOTS, slot):
                copy.start()

        return carry

    lax.fori_loop(0, tiles, step, 0)

    def project(n, dst):
        down(n).wait()

        def column(i, carry):
            at = pl.ds(pl.multiple_of(i * TILE, TILE), TILE)
            out = jnp.dot(hid[...], dbuf[n, :, at], preferred_element_type=F32)
            dst[:, at] = out.astype(dst.dtype)
            return carry

        lax.fori_loop(0, width // TILE, column, 0)

    project(0, c1_out)
    first_copy = send(c1_out, c1_in, {"tensor": core})
    project(1, acc)
    first_copy.wait_recv()
    x_out[...] = (acc[...] + c1_in[...].astype(F32)).astype(BF16)
    x_copy = send(x_out, x_in, {"tensor": across})
    project(2, c3_out)
    third_copy = send(c3_out, c3_in, {"tensor": core})
    project(3, acc)
    for copy in head_copies:
        copy.wait_recv()
    for h in range(4):
        attn_ref[:, h] = heads_in[h]
    third_copy.wait_recv()
    acc[...] = acc[...] + c3_in[...].astype(F32)
    x_copy.wait_recv()
    acc[...] = acc[...] + x_in[...].astype(F32)
    z_out[...] = acc[...].astype(BF16).reshape(pools, rows, width)
    last = []
    for j in (2, 1, 3):
        if j < pools:
            q = (p + j) % pools
            last.append(send(z_out.at[q], z_in.at[j], {"pool": q}))
    total = z_out[p].astype(F32)
    for copy in last:
        copy.wait_recv()
    for j in range(1, pools):
        total = total + z_in[j].astype(F32)
    comb_ref[...] = total.astype(BF16)
    for copy in sent:
        copy.wait_send()


def fused_shards(
    tokens, route_ids, route_weights, gate_weight, up_weight, down_weight,
    queries, keys, values, lengths,
):
    pools = lax.axis_size("pool")
    experts, model, ff = gate_weight.shape
    rows, width = tokens.shape
    units = experts * ff
    toks = pools * rows
    seqs, _, group, size = queries.shape
    gate_rows = jnp.swapaxes(gate_weight, 1, 2).reshape(units, model)
    up_rows = jnp.swapaxes(up_weight, 1, 2).reshape(units, model)
    down_rows = down_weight.reshape(units, model)
    copies = 3 * pools + 3 * (pools - 1) + 3 + 3
    vmem = pl.BlockSpec(memory_space=pltpu.VMEM)
    hbm = pl.BlockSpec(memory_space=pl.ANY)
    part = pltpu.VMEM((toks, width), BF16)
    return pl.pallas_call(
        functools.partial(kernel, experts),
        out_shape=(
            jax.ShapeDtypeStruct((seqs, 4, group, size), BF16),
            jax.ShapeDtypeStruct((rows, width), BF16),
        ),
        in_specs=[pl.BlockSpec(memory_space=pltpu.SMEM)] + [vmem] * 6 + [hbm] * 3,
        out_specs=(vmem, vmem),
        scratch_shapes=[
            pltpu.VMEM((4, pools, rows, width), BF16),
            pltpu.VMEM((pools, rows, 128), F32),
            pltpu.VMEM((pools, rows, 128), F32),
            pltpu.VMEM((seqs, group, size), BF16),
            pltpu.VMEM((4, seqs, group, size), BF16),
            pltpu.VMEM((SLOTS, TILE, model), BF16),
            pltpu.VMEM((SLOTS, TILE, model), BF16),
            pltpu.VMEM((4, units, width), BF16),
            pltpu.VMEM((toks, units), BF16),
            pltpu.VMEM((toks, width), F32),
            part, part, part, part, part, part,
            pltpu.VMEM((pools, rows, width), BF16),
            pltpu.VMEM((pools, rows, width), BF16),
            pltpu.SemaphoreType.DMA((2, SLOTS)),
            pltpu.SemaphoreType.DMA((4,)),
            pltpu.SemaphoreType.DMA((copies,)),
            pltpu.SemaphoreType.DMA((copies,)),
        ],
        compiler_params=pltpu.CompilerParams(
            collective_id=0, has_side_effects=True, vmem_limit_bytes=VMEM_LIMIT
        ),
        cost_estimate=pl.CostEstimate(
            flops=6 * toks * units * model,
            bytes_accessed=6 * units * model,
            transcendentals=toks * units,
        ),
    )(
        lengths, tokens, route_ids, route_weights,
        queries.reshape(seqs, group, size),
        keys.reshape(seqs, keys.shape[2], size),
        values.reshape(seqs, values.shape[2], size),
        gate_rows, up_rows, down_rows,
    )


def solution(mesh):
    in_specs = (
        P(("groups", "pool"), "tensor"),
        P(("groups", "pool"), None),
        P(("groups", "pool"), None),
        P("pool", None, "tensor"),
        P("pool", None, "tensor"),
        P("pool", "tensor", None),
        P(("groups", "pool"), "tensor", None, None),
        P(("groups", "pool"), "tensor", None, None),
        P(("groups", "pool"), "tensor", None, None),
        P(("groups", "pool")),
    )
    out_specs = (P(("groups", "pool"), None, None, None), P(("groups", "pool"), "tensor"))
    fused = mesh.shape["tensor"] == 4 and mesh.shape["pool"] == 4
    shards = fused_shards if fused else routed_shards
    return jax.shard_map(shards, mesh=mesh, in_specs=in_specs, out_specs=out_specs, check_vma=False)
```

```python
import functools

import jax
import jax.numpy as jnp
from jax import lax
from jax.experimental import pallas as pl
from jax.experimental.pallas import tpu as pltpu
from jax.sharding import PartitionSpec as P

CAP = 6
TILE = 256
SPARE = 2
F32 = jnp.float32
BF16 = jnp.bfloat16
VMEM_LIMIT = 60 * 1024 * 1024


def attend(queries, keys, values, lengths):
    scale = queries.shape[-1] ** (-0.5)
    scores = (
        jnp.einsum("sjgh,sjch->sjgc", queries, keys, preferred_element_type=jnp.float32) * scale
    )
    position = lax.broadcasted_iota(jnp.int32, (keys.shape[0], keys.shape[2]), 1)
    live = position < lengths[:, None]
    scores = jnp.where(live[:, None, None, :], scores, -1e30)
    highest = jnp.max(scores, axis=3, keepdims=True)
    probs = jnp.exp(scores - highest)
    weights = (probs / jnp.sum(probs, axis=3, keepdims=True)).astype(jnp.bfloat16)
    mixed = jnp.einsum("sjgc,sjch->sjgh", weights, values, preferred_element_type=jnp.float32)
    return mixed.astype(jnp.bfloat16)


def slot_table(route_ids, experts, capacity):
    flat_ids = route_ids.reshape(-1)
    count = flat_ids.shape[0]
    onehot = (flat_ids[:, None] == lax.broadcasted_iota(jnp.int32, (1, experts), 1)).astype(
        jnp.int32
    )
    before = jnp.cumsum(onehot, axis=0) - onehot
    rank = jnp.sum(before * onehot, axis=1)
    slot = flat_ids * capacity + rank
    owner = lax.broadcasted_iota(jnp.int32, (count,), 0) // route_ids.shape[1]
    source = jnp.full((experts * capacity,), -1, jnp.int32).at[slot].set(owner)
    return (slot, source)


def routed_shards(
    tokens, route_ids, route_weights, gate_weight, up_weight, down_weight,
    queries, keys, values, lengths,
):
    local_heads = attend(queries, keys, values, lengths)
    attention = lax.all_gather(local_heads, "tensor", axis=1, tiled=True)
    pool_size = lax.axis_size("pool")
    local_experts = gate_weight.shape[0]
    experts = local_experts * pool_size
    slot, source = slot_table(route_ids, experts, CAP)
    filled = (source >= 0)[:, None]
    picked = jnp.maximum(source, 0)
    whole = lax.all_gather(tokens, "tensor", axis=1, tiled=True)
    outgoing = jnp.where(filled, whole[picked], jnp.zeros((), whole.dtype))
    outgoing = outgoing.reshape(pool_size, local_experts, CAP, whole.shape[1])
    arrived = lax.all_to_all(outgoing, "pool", split_axis=0, concat_axis=0, tiled=True)
    gate = jnp.einsum("pech,ehf->pecf", arrived, gate_weight, preferred_element_type=jnp.float32)
    up = jnp.einsum("pech,ehf->pecf", arrived, up_weight, preferred_element_type=jnp.float32)
    hidden = (jax.nn.silu(gate) * up).astype(jnp.bfloat16)
    partial_value = jnp.einsum(
        "pecf,efd->pecd", hidden, down_weight, preferred_element_type=jnp.float32
    )
    summed = lax.psum_scatter(
        partial_value.astype(jnp.bfloat16), "tensor", scatter_dimension=3, tiled=True
    )
    returned = lax.all_to_all(summed, "pool", split_axis=0, concat_axis=0, tiled=True)
    fetched = returned.reshape(experts * CAP, returned.shape[3])[slot]
    fetched = fetched.reshape(route_ids.shape[0], route_ids.shape[1], returned.shape[3])
    combined = jnp.sum(fetched.astype(jnp.float32) * route_weights[:, :, None], axis=1)
    return (attention, combined.astype(jnp.bfloat16))


def kernel(
    experts, len_ref, tok_hbm, ids_ref, rw_ref, q_hbm, k_hbm, v_hbm, gate_hbm, up_hbm, down_hbm,
    attn_ref, comb_ref,
    x, tab_out, tab_in, table, q_buf, k_buf, v_buf, heads_own, heads_in, ring, hid, acc,
    c1_out, c1_in, x_out, x_in, c3_out, c3_in, z_out, z_in,
    w_sem, l_sem, s_sem, r_sem,
):
    pools, rows, width = x.shape[1:]
    toks = pools * rows
    units = gate_hbm.shape[0]
    ff = units // experts
    tiles = units // TILE
    slots = ring.shape[0]
    spare = slots - 2 * tiles
    p = lax.axis_index("pool")
    t = lax.axis_index("tensor")
    core = t + 1 - 2 * (t % 2)
    across = (t + 2) % 4
    corner = (core + 2) % 4
    blocks = (corner, across, core, t)
    near = [j for j in (1, 3, 2) if j < pools]
    far = [j for j in (2, 1, 3) if j < pools]

    barrier = pltpu.get_barrier_semaphore()
    for j in range(1, pools):
        pl.semaphore_signal(barrier, inc=1, device_id={"pool": (p + j) % pools})
    for j in range(1, 4):
        pl.semaphore_signal(barrier, inc=1, device_id={"tensor": (t + j) % 4})

    def weight(src, i, slot):
        at = pl.ds(pl.multiple_of(i * TILE, TILE), TILE)
        return pltpu.make_async_copy(src.at[at], ring.at[slot], w_sem.at[slot])

    own = pltpu.make_async_copy(tok_hbm, x.at[t, p], l_sem.at[0])
    own.start()
    for i in range(tiles):
        weight(gate_hbm, i, 2 * i).start()
        weight(up_hbm, i, 2 * i + 1).start()
        if i == 1:
            pl.semaphore_wait(barrier, pools + 2)
            count = [0]
            sent = []

            def send(src, dst, where):
                n = count[0]
                count[0] = n + 1
                copy = pltpu.make_async_remote_copy(
                    src_ref=src, dst_ref=dst, send_sem=s_sem.at[n], recv_sem=r_sem.at[n],
                    device_id=where,
                )
                copy.start()
                sent.append(copy)
                return copy

            mine = x.at[t, p]
            z_copies = {}
            for j in far:
                z_copies[j] = send(tok_hbm, mine, {"pool": (p + pools - j) % pools})
            x_copies = [send(tok_hbm, mine, {"tensor": across})]
            core_copies = [send(tok_hbm, mine, {"tensor": core})]
    for i in range(spare):
        weight(down_hbm, i, 2 * tiles + i).start()
    loads = [
        pltpu.make_async_copy(src, dst, l_sem.at[n + 1])
        for n, (src, dst) in enumerate(((q_hbm, q_buf), (k_hbm, k_buf), (v_hbm, v_buf)))
    ]
    for copy in loads:
        copy.start()

    expert = lax.broadcasted_iota(jnp.int32, (experts, rows), 0)
    tab_copies = []
    for j in far + [0]:
        owner = (p + pools - j) % pools
        total = jnp.zeros((experts, rows), F32)
        for k in range(ids_ref.shape[0]):
            hit = (ids_ref[k : k + 1, :] - owner * experts) == expert
            total = total + jnp.where(hit, rw_ref[k : k + 1, :], 0.0)
        if j == 0:
            tab_in[p] = total
        else:
            tab_out[j] = total
            tab_copies.append(send(tab_out.at[j], tab_in.at[p], {"pool": owner}))

    for j in near:
        z_copies[j].wait_recv()
        block = x.at[t, (p + j) % pools]
        x_copies.append(send(block, block, {"tensor": across}))
        core_copies.append(send(block, block, {"tensor": core}))
    for n, j in enumerate([0] + near):
        x_copies[n].wait_recv()
        block = x.at[across, (p + j) % pools]
        core_copies.append(send(block, block, {"tensor": core}))
    for copy in tab_copies:
        copy.wait_recv()
    table[...] = jnp.concatenate([tab_in[n] for n in range(pools)], axis=1)
    own.wait()
    for copy in core_copies:
        copy.wait_recv()

    unit = lax.broadcasted_iota(jnp.int32, (TILE, toks), 0)
    dims = (((1,), (1,)), ((), ()))

    def step(i, carry):
        weight(gate_hbm, i, 2 * i).wait()
        weight(up_hbm, i, 2 * i + 1).wait()
        gate = jnp.zeros((TILE, toks), F32)
        up = jnp.zeros((TILE, toks), F32)
        for b in range(4):
            xb = x[b].reshape(toks, width)
            at = slice(b * width, (b + 1) * width)
            gate = gate + lax.dot_general(
                ring[2 * i, :, at], xb, dims, preferred_element_type=F32
            )
            up = up + lax.dot_general(
                ring[2 * i + 1, :, at], xb, dims, preferred_element_type=F32
            )
        first = (i * TILE) // ff
        share = jnp.zeros((TILE, toks), F32)
        for m in range((TILE - 2) // ff + 2):
            e = first + m
            row = table[pl.ds(jnp.minimum(e, experts - 1), 1), :]
            inside = (unit >= e * ff - i * TILE) & (unit < (e + 1) * ff - i * TILE)
            share = jnp.where(inside, row, share)
        value = gate / (1.0 + jnp.exp(-gate)) * up * share
        hid[:, pl.ds(pl.multiple_of(i * TILE, TILE), TILE)] = value.T.astype(BF16)

        for m in range(2):

            @pl.when(spare + 2 * i + m < tiles)
            def _():
                weight(down_hbm, spare + 2 * i + m, 2 * i + m).start()

        return carry

    lax.fori_loop(0, tiles, step, 0)

    places = [2 * tiles + j if j < spare else j - spare for j in range(tiles)]
    for j in range(tiles):
        weight(down_hbm, j, places[j]).wait()

    def project(n, dst):
        def column(i, carry):
            at = pl.ds(pl.multiple_of(blocks[n] * width + i * TILE, TILE), TILE)
            out = jnp.zeros((toks, TILE), F32)
            for j in range(tiles):
                out = out + jnp.dot(
                    hid[:, j * TILE : (j + 1) * TILE], ring[places[j], :, at],
                    preferred_element_type=F32,
                )
            dst[:, pl.ds(pl.multiple_of(i * TILE, TILE), TILE)] = out.astype(dst.dtype)
            return carry

        lax.fori_loop(0, width // TILE, column, 0)

    def rows_of(ref, q):
        return ref.at[pl.ds(pl.multiple_of(q * rows, rows), rows)]

    project(0, c1_out)
    first_copy = send(c1_out, c1_in, {"tensor": core})
    project(1, acc)
    first_copy.wait_recv()
    back = {}
    for j in far + [0]:
        q = (p + j) % pools
        piece = rows_of(acc, q)[...] + rows_of(c1_in, q)[...].astype(F32)
        rows_of(x_out, q)[...] = piece.astype(BF16)
        back[j] = send(rows_of(x_out, q), rows_of(x_in, q), {"tensor": across})
    project(2, c3_out)
    third_copy = send(c3_out, c3_in, {"tensor": core})
    project(3, acc)

    for copy in loads:
        copy.wait()
    scale = q_buf.shape[-1] ** (-0.5)
    for s in range(q_buf.shape[0]):
        scores = lax.dot_general(q_buf[s], k_buf[s], dims, preferred_element_type=F32) * scale
        position = lax.broadcasted_iota(jnp.int32, scores.shape, 1)
        scores = jnp.where(position < len_ref[s], scores, -1e30)
        probs = jnp.exp(scores - jnp.max(scores, axis=1, keepdims=True))
        mix = (probs / jnp.sum(probs, axis=1, keepdims=True)).astype(BF16)
        heads_own[s] = jnp.dot(mix, v_buf[s], preferred_element_type=F32).astype(BF16)
    heads_in[t] = heads_own[...]
    head_copies = [
        send(heads_own, heads_in.at[t], {"tensor": (t + j) % 4}) for j in range(1, 4)
    ]

    third_copy.wait_recv()
    last = []
    for j in far + [0]:
        q = (p + j) % pools
        back[j].wait_recv()
        piece = (
            rows_of(acc, q)[...]
            + rows_of(c3_in, q)[...].astype(F32)
            + rows_of(x_in, q)[...].astype(F32)
        )
        if j == 0:
            total = piece
        else:
            z_out[j] = piece.astype(BF16)
            last.append(send(z_out.at[j], z_in.at[j], {"pool": q}))
    for copy in head_copies:
        copy.wait_recv()
    for h in range(4):
        attn_ref[:, h] = heads_in[h]
    for copy in last:
        copy.wait_recv()
    for j in range(1, pools):
        total = total + z_in[j].astype(F32)
    comb_ref[...] = total.astype(BF16)
    for copy in sent:
        copy.wait_send()


def fused_shards(
    tokens, route_ids, route_weights, gate_weight, up_weight, down_weight,
    queries, keys, values, lengths,
):
    pools = lax.axis_size("pool")
    experts, model, ff = gate_weight.shape
    rows, width = tokens.shape
    units = experts * ff
    toks = pools * rows
    seqs, _, group, size = queries.shape
    ctx = keys.shape[2]
    gate_rows = jnp.swapaxes(gate_weight, 1, 2).reshape(units, model)
    up_rows = jnp.swapaxes(up_weight, 1, 2).reshape(units, model)
    down_rows = down_weight.reshape(units, model)
    copies = 3 * pools + 2 * (pools - 1) + 3 + 2 + pools + pools
    vmem = pl.BlockSpec(memory_space=pltpu.VMEM)
    hbm = pl.BlockSpec(memory_space=pl.ANY)
    part = pltpu.VMEM((toks, width), BF16)
    return pl.pallas_call(
        functools.partial(kernel, experts),
        out_shape=(
            jax.ShapeDtypeStruct((seqs, 4, group, size), BF16),
            jax.ShapeDtypeStruct((rows, width), BF16),
        ),
        in_specs=[pl.BlockSpec(memory_space=pltpu.SMEM), hbm, vmem, vmem] + [hbm] * 6,
        out_specs=(vmem, vmem),
        scratch_shapes=[
            pltpu.VMEM((4, pools, rows, width), BF16),
            pltpu.VMEM((pools, experts, rows), F32),
            pltpu.VMEM((pools, experts, rows), F32),
            pltpu.VMEM((experts, toks), F32),
            pltpu.VMEM((seqs, group, size), BF16),
            pltpu.VMEM((seqs, ctx, size), BF16),
            pltpu.VMEM((seqs, ctx, size), BF16),
            pltpu.VMEM((seqs, group, size), BF16),
            pltpu.VMEM((4, seqs, group, size), BF16),
            pltpu.VMEM((2 * (units // TILE) + SPARE, TILE, model), BF16),
            pltpu.VMEM((toks, units), BF16),
            pltpu.VMEM((toks, width), F32),
            part, part, part, part, part, part,
            pltpu.VMEM((pools, rows, width), BF16),
            pltpu.VMEM((pools, rows, width), BF16),
            pltpu.SemaphoreType.DMA((2 * (units // TILE) + SPARE,)),
            pltpu.SemaphoreType.DMA((4,)),
            pltpu.SemaphoreType.DMA((copies,)),
            pltpu.SemaphoreType.DMA((copies,)),
        ],
        compiler_params=pltpu.CompilerParams(
            collective_id=0, has_side_effects=True, vmem_limit_bytes=VMEM_LIMIT
        ),
        cost_estimate=pl.CostEstimate(
            flops=6 * toks * units * model,
            bytes_accessed=6 * units * model,
            transcendentals=toks * units,
        ),
    )(
        lengths, tokens, route_ids.T, route_weights.T,
        queries.reshape(seqs, group, size),
        keys.reshape(seqs, ctx, size),
        values.reshape(seqs, ctx, size),
        gate_rows, up_rows, down_rows,
    )


def solution(mesh):
    in_specs = (
        P(("groups", "pool"), "tensor"),
        P(("groups", "pool"), None),
        P(("groups", "pool"), None),
        P("pool", None, "tensor"),
        P("pool", None, "tensor"),
        P("pool", "tensor", None),
        P(("groups", "pool"), "tensor", None, None),
        P(("groups", "pool"), "tensor", None, None),
        P(("groups", "pool"), "tensor", None, None),
        P(("groups", "pool")),
    )
    out_specs = (P(("groups", "pool"), None, None, None), P(("groups", "pool"), "tensor"))
    fused = mesh.shape["tensor"] == 4 and mesh.shape["pool"] == 4
    shards = fused_shards if fused else routed_shards
    return jax.shard_map(shards, mesh=mesh, in_specs=in_specs, out_specs=out_specs, check_vma=False)
```

```python
import functools

import jax
import jax.numpy as jnp
from jax import lax
from jax.experimental import pallas as pl
from jax.experimental.pallas import tpu as pltpu
from jax.sharding import PartitionSpec as P

CAP = 6
TILE = 256
SPARE = 2
PAIR = 2
WIDE = 512
F32 = jnp.float32
BF16 = jnp.bfloat16
VMEM_LIMIT = 60 * 1024 * 1024


def attend(queries, keys, values, lengths):
    scale = queries.shape[-1] ** (-0.5)
    scores = (
        jnp.einsum("sjgh,sjch->sjgc", queries, keys, preferred_element_type=jnp.float32) * scale
    )
    position = lax.broadcasted_iota(jnp.int32, (keys.shape[0], keys.shape[2]), 1)
    live = position < lengths[:, None]
    scores = jnp.where(live[:, None, None, :], scores, -1e30)
    highest = jnp.max(scores, axis=3, keepdims=True)
    probs = jnp.exp(scores - highest)
    weights = (probs / jnp.sum(probs, axis=3, keepdims=True)).astype(jnp.bfloat16)
    mixed = jnp.einsum("sjgc,sjch->sjgh", weights, values, preferred_element_type=jnp.float32)
    return mixed.astype(jnp.bfloat16)


def slot_table(route_ids, experts, capacity):
    flat_ids = route_ids.reshape(-1)
    count = flat_ids.shape[0]
    onehot = (flat_ids[:, None] == lax.broadcasted_iota(jnp.int32, (1, experts), 1)).astype(
        jnp.int32
    )
    before = jnp.cumsum(onehot, axis=0) - onehot
    rank = jnp.sum(before * onehot, axis=1)
    slot = flat_ids * capacity + rank
    owner = lax.broadcasted_iota(jnp.int32, (count,), 0) // route_ids.shape[1]
    source = jnp.full((experts * capacity,), -1, jnp.int32).at[slot].set(owner)
    return (slot, source)


def routed_shards(
    tokens, route_ids, route_weights, gate_weight, up_weight, down_weight,
    queries, keys, values, lengths,
):
    local_heads = attend(queries, keys, values, lengths)
    attention = lax.all_gather(local_heads, "tensor", axis=1, tiled=True)
    pool_size = lax.axis_size("pool")
    local_experts = gate_weight.shape[0]
    experts = local_experts * pool_size
    slot, source = slot_table(route_ids, experts, CAP)
    filled = (source >= 0)[:, None]
    picked = jnp.maximum(source, 0)
    whole = lax.all_gather(tokens, "tensor", axis=1, tiled=True)
    outgoing = jnp.where(filled, whole[picked], jnp.zeros((), whole.dtype))
    outgoing = outgoing.reshape(pool_size, local_experts, CAP, whole.shape[1])
    arrived = lax.all_to_all(outgoing, "pool", split_axis=0, concat_axis=0, tiled=True)
    gate = jnp.einsum("pech,ehf->pecf", arrived, gate_weight, preferred_element_type=jnp.float32)
    up = jnp.einsum("pech,ehf->pecf", arrived, up_weight, preferred_element_type=jnp.float32)
    hidden = (jax.nn.silu(gate) * up).astype(jnp.bfloat16)
    partial_value = jnp.einsum(
        "pecf,efd->pecd", hidden, down_weight, preferred_element_type=jnp.float32
    )
    summed = lax.psum_scatter(
        partial_value.astype(jnp.bfloat16), "tensor", scatter_dimension=3, tiled=True
    )
    returned = lax.all_to_all(summed, "pool", split_axis=0, concat_axis=0, tiled=True)
    fetched = returned.reshape(experts * CAP, returned.shape[3])[slot]
    fetched = fetched.reshape(route_ids.shape[0], route_ids.shape[1], returned.shape[3])
    combined = jnp.sum(fetched.astype(jnp.float32) * route_weights[:, :, None], axis=1)
    return (attention, combined.astype(jnp.bfloat16))


def kernel(
    experts, len_ref, tok_hbm, ids_ref, rw_ref, q_hbm, k_hbm, v_hbm, gate_hbm, up_hbm, down_hbm,
    attn_ref, comb_ref,
    x, tab_out, tab_in, table, q_buf, k_buf, v_buf, heads_own, heads_in, ring, hid, acc,
    c1_out, c1_in, x_out, x_in, c3_out, c3_in, z_out, z_in,
    w_sem, l_sem, s_sem, r_sem,
):
    pools, rows, width = x.shape[1:]
    toks = pools * rows
    units = gate_hbm.shape[0]
    ff = units // experts
    tiles = units // TILE
    slots = ring.shape[0]
    spare = slots - 2 * tiles
    p = lax.axis_index("pool")
    t = lax.axis_index("tensor")
    core = t + 1 - 2 * (t % 2)
    across = (t + 2) % 4
    corner = (core + 2) % 4
    blocks = (corner, across, core, t)
    near = [j for j in (1, 3, 2) if j < pools]
    far = [j for j in (2, 1, 3) if j < pools]

    barrier = pltpu.get_barrier_semaphore()
    for j in range(1, pools):
        pl.semaphore_signal(barrier, inc=1, device_id={"pool": (p + j) % pools})
    for j in range(1, 4):
        pl.semaphore_signal(barrier, inc=1, device_id={"tensor": (t + j) % 4})

    def weight(src, i, slot):
        at = pl.ds(pl.multiple_of(i * TILE, TILE), TILE)
        return pltpu.make_async_copy(src.at[at], ring.at[slot], w_sem.at[slot])

    own = pltpu.make_async_copy(tok_hbm, x.at[t, p], l_sem.at[0])
    own.start()
    for i in range(tiles):
        weight(gate_hbm, i, 2 * i).start()
        weight(up_hbm, i, 2 * i + 1).start()
        if i == 1:
            pl.semaphore_wait(barrier, pools + 2)
            count = [0]
            sent = []

            def send(src, dst, where):
                n = count[0]
                count[0] = n + 1
                copy = pltpu.make_async_remote_copy(
                    src_ref=src, dst_ref=dst, send_sem=s_sem.at[n], recv_sem=r_sem.at[n],
                    device_id=where,
                )
                copy.start()
                sent.append(copy)
                return copy

            mine = x.at[t, p]
            z_copies = {}
            for j in far:
                z_copies[j] = send(tok_hbm, mine, {"pool": (p + pools - j) % pools})
            x_copies = [send(tok_hbm, mine, {"tensor": across})]
            core_copies = [send(tok_hbm, mine, {"tensor": core})]
    for i in range(spare):
        weight(down_hbm, i, 2 * tiles + i).start()
    loads = [
        pltpu.make_async_copy(src, dst, l_sem.at[n + 1])
        for n, (src, dst) in enumerate(((q_hbm, q_buf), (k_hbm, k_buf), (v_hbm, v_buf)))
    ]
    for copy in loads:
        copy.start()

    expert = lax.broadcasted_iota(jnp.int32, (experts, rows), 0)
    tab_copies = []
    for j in far + [0]:
        owner = (p + pools - j) % pools
        total = jnp.zeros((experts, rows), F32)
        for k in range(ids_ref.shape[0]):
            hit = (ids_ref[k : k + 1, :] - owner * experts) == expert
            total = total + jnp.where(hit, rw_ref[k : k + 1, :], 0.0)
        if j == 0:
            tab_in[p] = total
        else:
            tab_out[j] = total
            tab_copies.append(send(tab_out.at[j], tab_in.at[p], {"pool": owner}))

    for j in near:
        z_copies[j].wait_recv()
        block = x.at[t, (p + j) % pools]
        x_copies.append(send(block, block, {"tensor": across}))
        core_copies.append(send(block, block, {"tensor": core}))
    for n, j in enumerate([0] + near):
        x_copies[n].wait_recv()
        block = x.at[across, (p + j) % pools]
        core_copies.append(send(block, block, {"tensor": core}))
    for copy in tab_copies:
        copy.wait_recv()
    table[...] = jnp.concatenate([tab_in[n] for n in range(pools)], axis=1)
    own.wait()
    for copy in core_copies:
        copy.wait_recv()

    unit = lax.broadcasted_iota(jnp.int32, (TILE, toks), 0)
    dims = (((1,), (1,)), ((), ()))

    def tile(i):
        gate = jnp.zeros((TILE, toks), F32)
        up = jnp.zeros((TILE, toks), F32)
        for b in range(4):
            xb = x[b].reshape(toks, width)
            at = slice(b * width, (b + 1) * width)
            gate = gate + lax.dot_general(
                ring[2 * i, :, at], xb, dims, preferred_element_type=F32
            )
            up = up + lax.dot_general(
                ring[2 * i + 1, :, at], xb, dims, preferred_element_type=F32
            )
        first = (i * TILE) // ff
        share = jnp.zeros((TILE, toks), F32)
        for m in range((TILE - 2) // ff + 2):
            e = first + m
            row = table[pl.ds(jnp.minimum(e, experts - 1), 1), :]
            inside = (unit >= e * ff - i * TILE) & (unit < (e + 1) * ff - i * TILE)
            share = jnp.where(inside, row, share)
        value = gate / (1.0 + jnp.exp(-gate)) * up * share
        return value.T.astype(BF16)

    def step(n, carry):
        for m in range(PAIR):
            weight(gate_hbm, PAIR * n + m, 2 * (PAIR * n + m)).wait()
            weight(up_hbm, PAIR * n + m, 2 * (PAIR * n + m) + 1).wait()
        values = [tile(PAIR * n + m) for m in range(PAIR)]
        for m in range(PAIR):
            at = pl.multiple_of((PAIR * n + m) * TILE, TILE)
            hid[:, pl.ds(at, TILE)] = values[m]
        for m in range(2 * PAIR):

            @pl.when(spare + 2 * PAIR * n + m < tiles)
            def _():
                weight(down_hbm, spare + 2 * PAIR * n + m, 2 * PAIR * n + m).start()

        return carry

    lax.fori_loop(0, tiles // PAIR, step, 0)

    places = [2 * tiles + j if j < spare else j - spare for j in range(tiles)]
    for j in range(tiles):
        weight(down_hbm, j, places[j]).wait()

    def project(n, dst):
        def column(i, carry):
            at = pl.ds(pl.multiple_of(blocks[n] * width + i * WIDE, WIDE), WIDE)
            out = jnp.zeros((toks, WIDE), F32)
            for j in range(tiles):
                out = out + jnp.dot(
                    hid[:, j * TILE : (j + 1) * TILE], ring[places[j], :, at],
                    preferred_element_type=F32,
                )
            dst[:, pl.ds(pl.multiple_of(i * WIDE, WIDE), WIDE)] = out.astype(dst.dtype)
            return carry

        lax.fori_loop(0, width // WIDE, column, 0)

    def rows_of(ref, q):
        return ref.at[pl.ds(pl.multiple_of(q * rows, rows), rows)]

    project(0, c1_out)
    first_copy = send(c1_out, c1_in, {"tensor": core})
    project(1, acc)
    first_copy.wait_recv()
    back = {}
    for j in far + [0]:
        q = (p + j) % pools
        piece = rows_of(acc, q)[...] + rows_of(c1_in, q)[...].astype(F32)
        rows_of(x_out, q)[...] = piece.astype(BF16)
        back[j] = send(rows_of(x_out, q), rows_of(x_in, q), {"tensor": across})
    project(2, c3_out)
    third_copy = send(c3_out, c3_in, {"tensor": core})
    project(3, acc)

    for copy in loads:
        copy.wait()
    scale = q_buf.shape[-1] ** (-0.5)
    for s in range(q_buf.shape[0]):
        scores = lax.dot_general(q_buf[s], k_buf[s], dims, preferred_element_type=F32) * scale
        position = lax.broadcasted_iota(jnp.int32, scores.shape, 1)
        scores = jnp.where(position < len_ref[s], scores, -1e30)
        probs = jnp.exp(scores - jnp.max(scores, axis=1, keepdims=True))
        mix = (probs / jnp.sum(probs, axis=1, keepdims=True)).astype(BF16)
        heads_own[s] = jnp.dot(mix, v_buf[s], preferred_element_type=F32).astype(BF16)
    heads_in[t] = heads_own[...]
    head_copies = [
        send(heads_own, heads_in.at[t], {"tensor": (t + j) % 4}) for j in range(1, 4)
    ]

    third_copy.wait_recv()
    last = []
    for j in far + [0]:
        q = (p + j) % pools
        back[j].wait_recv()
        piece = (
            rows_of(acc, q)[...]
            + rows_of(c3_in, q)[...].astype(F32)
            + rows_of(x_in, q)[...].astype(F32)
        )
        if j == 0:
            total = piece
        else:
            z_out[j] = piece.astype(BF16)
            last.append(send(z_out.at[j], z_in.at[j], {"pool": q}))
    for copy in head_copies:
        copy.wait_recv()
    for h in range(4):
        attn_ref[:, h] = heads_in[h]
    for copy in last:
        copy.wait_recv()
    for j in range(1, pools):
        total = total + z_in[j].astype(F32)
    comb_ref[...] = total.astype(BF16)
    for copy in sent:
        copy.wait_send()


def fused_shards(
    tokens, route_ids, route_weights, gate_weight, up_weight, down_weight,
    queries, keys, values, lengths,
):
    pools = lax.axis_size("pool")
    experts, model, ff = gate_weight.shape
    rows, width = tokens.shape
    units = experts * ff
    toks = pools * rows
    seqs, _, group, size = queries.shape
    ctx = keys.shape[2]
    gate_rows = jnp.swapaxes(gate_weight, 1, 2).reshape(units, model)
    up_rows = jnp.swapaxes(up_weight, 1, 2).reshape(units, model)
    down_rows = down_weight.reshape(units, model)
    copies = 3 * pools + 2 * (pools - 1) + 3 + 2 + pools + pools
    vmem = pl.BlockSpec(memory_space=pltpu.VMEM)
    hbm = pl.BlockSpec(memory_space=pl.ANY)
    part = pltpu.VMEM((toks, width), BF16)
    return pl.pallas_call(
        functools.partial(kernel, experts),
        out_shape=(
            jax.ShapeDtypeStruct((seqs, 4, group, size), BF16),
            jax.ShapeDtypeStruct((rows, width), BF16),
        ),
        in_specs=[pl.BlockSpec(memory_space=pltpu.SMEM), hbm, vmem, vmem] + [hbm] * 6,
        out_specs=(vmem, vmem),
        scratch_shapes=[
            pltpu.VMEM((4, pools, rows, width), BF16),
            pltpu.VMEM((pools, experts, rows), F32),
            pltpu.VMEM((pools, experts, rows), F32),
            pltpu.VMEM((experts, toks), F32),
            pltpu.VMEM((seqs, group, size), BF16),
            pltpu.VMEM((seqs, ctx, size), BF16),
            pltpu.VMEM((seqs, ctx, size), BF16),
            pltpu.VMEM((seqs, group, size), BF16),
            pltpu.VMEM((4, seqs, group, size), BF16),
            pltpu.VMEM((2 * (units // TILE) + SPARE, TILE, model), BF16),
            pltpu.VMEM((toks, units), BF16),
            pltpu.VMEM((toks, width), F32),
            part, part, part, part, part, part,
            pltpu.VMEM((pools, rows, width), BF16),
            pltpu.VMEM((pools, rows, width), BF16),
            pltpu.SemaphoreType.DMA((2 * (units // TILE) + SPARE,)),
            pltpu.SemaphoreType.DMA((4,)),
            pltpu.SemaphoreType.DMA((copies,)),
            pltpu.SemaphoreType.DMA((copies,)),
        ],
        compiler_params=pltpu.CompilerParams(
            collective_id=0, has_side_effects=True, vmem_limit_bytes=VMEM_LIMIT
        ),
        cost_estimate=pl.CostEstimate(
            flops=6 * toks * units * model,
            bytes_accessed=6 * units * model,
            transcendentals=toks * units,
        ),
    )(
        lengths, tokens, route_ids.T, route_weights.T,
        queries.reshape(seqs, group, size),
        keys.reshape(seqs, ctx, size),
        values.reshape(seqs, ctx, size),
        gate_rows, up_rows, down_rows,
    )


def solution(mesh):
    in_specs = (
        P(("groups", "pool"), "tensor"),
        P(("groups", "pool"), None),
        P(("groups", "pool"), None),
        P("pool", None, "tensor"),
        P("pool", None, "tensor"),
        P("pool", "tensor", None),
        P(("groups", "pool"), "tensor", None, None),
        P(("groups", "pool"), "tensor", None, None),
        P(("groups", "pool"), "tensor", None, None),
        P(("groups", "pool")),
    )
    out_specs = (P(("groups", "pool"), None, None, None), P(("groups", "pool"), "tensor"))
    fused = mesh.shape["tensor"] == 4 and mesh.shape["pool"] == 4
    shards = fused_shards if fused else routed_shards
    return jax.shard_map(shards, mesh=mesh, in_specs=in_specs, out_specs=out_specs, check_vma=False)
```
